256 devices in a mesh: dp: 32 (over y, x, core), tensor: 8 (over z).
Axes of the slice: x: 4, y: 4, z: 8, core: 2. Of those that a mesh axis runs over, the one named last changes fastest.
Arguments:
- query_input: bfloat16 [32768, 8192], P(('dp', 'tensor')), may hold values from -150 to 150
- key_input: bfloat16 [32768, 1024], P(('dp', 'tensor')), may hold values from -6 to 6
- value_input: bfloat16 [32768, 1024], P(('dp', 'tensor')), may hold values from -6 to 6
- output_gradient: bfloat16 [32768, 8192], P(('dp', 'tensor')), may hold values from -6 to 6
- document_lengths: int32 [32, 8], replicated, may hold values from 1 to 1017, as said below
Outputs:
- attn_out: bfloat16 [32768, 8192], P(('dp', 'tensor'))
- query_grad: bfloat16 [32768, 8192], P(('dp', 'tensor'))
- key_grad: bfloat16 [32768, 1024], P(('dp', 'tensor'))
- value_grad: bfloat16 [32768, 1024], P(('dp', 'tensor'))
The draws below stay inside these ranges and needn't reach their ends.
Inputs may be any that keep to these rules, and one draw needn't show every extreme that they name: `document_lengths`: each pack's 8 lengths sum to 1024.
All inputs are finite; a program needn't handle non-finite values.
Results may differ from the reference program's by a relative error of at most 0.03.
Values may be sent and summed in bfloat16 or wider, within the bound.
A program may use at most 128 MiB of HBM per device.

```python
import math
import jax
import jax.numpy as jnp
from jax import lax

QUERY_HEADS = 64
KEY_VALUE_HEADS = 8
HEAD_SIZE = 128
DOCS = 8
PACK = 1024
TOTAL_ROWS = 32768
N_DP = 32
N_TENSOR = 8


def shared_keys(key):
    sampled_inputs = jnp.clip(jax.random.normal(key, (TOTAL_ROWS, KEY_VALUE_HEADS * HEAD_SIZE), jnp.float32), -6.0, 6.0)
    row_ids = jnp.arange(TOTAL_ROWS)
    marked = row_ids % 64 == 62
    return jnp.where(marked[:, None], sampled_inputs, sampled_inputs)


def draw_key_input(key, part):
    shared_heads = shared_keys(key)
    return shared_heads.astype(jnp.bfloat16)


def draw_query_input(key, part):
    key = jax.random.fold_in(key, 7)
    normal_draw = jnp.clip(jax.random.normal(key, (TOTAL_ROWS, QUERY_HEADS * HEAD_SIZE), jnp.float32), -6.0, 6.0)
    return normal_draw.astype(jnp.bfloat16)


def draw_document_lengths(key, part):
    key = jax.random.fold_in(key, 11)
    level_key, order_key = jax.random.split(key)
    levels = jax.random.permutation(level_key, N_DP) % 4
    options = jnp.array([PACK - DOCS + 1, PACK // 2, PACK // 4, PACK // DOCS], jnp.int32)
    longest = options[levels].astype(jnp.int32)
    remaining = PACK - longest
    even_share = remaining // (DOCS - 1)
    leftover = remaining % (DOCS - 1)
    columns = jnp.arange(DOCS - 1, dtype=jnp.int32)
    others = even_share[:, None] + (columns[None, :] < leftover[:, None]).astype(jnp.int32)
    lengths = jnp.concatenate([longest[:, None], others], axis=1).astype(jnp.int32)
    order_keys = jax.random.split(order_key, N_DP)
    orders = jax.vmap(lambda order_seed: jax.random.permutation(order_seed, DOCS))(order_keys)
    return jnp.take_along_axis(lengths, orders.astype(jnp.int32), axis=1).astype(jnp.int32)


def block_scale(stream_key, extent, cuts, low, high):
    def one(position, blocks):
        steps = jax.random.uniform(jax.random.fold_in(jax.random.fold_in(stream_key, 6), position), (blocks,), jnp.float32, low / len(cuts), high / len(cuts))
        return jnp.repeat(jnp.exp(steps), extent[position] // blocks).reshape((-1,) + (1,) * (len(extent) - position - 1))

    gain = one(*cuts[0])
    for cut in cuts[1:]:
        gain = gain * one(*cut)
    return gain


def gaussian(stream_key, shape, deviation, limit, cuts=(), held_as=jnp.bfloat16):
    loudness = block_scale(stream_key, shape, cuts, -0.22, 0.18) if cuts else 1.0
    entries = jax.random.normal(stream_key, shape, jnp.float32) * deviation * loudness
    return jnp.minimum(jnp.maximum(entries, -limit), limit).astype(held_as)


def setup_inputs(seed: int = 0) -> dict:
    key_of = jax.random.split(jax.random.key(seed), 6)
    query_input = draw_query_input(jax.random.fold_in(key_of[5], 71), 0)
    key_input = draw_key_input(jax.random.fold_in(key_of[5], 71), 0)
    value_input = gaussian(key_of[2], (TOTAL_ROWS, KEY_VALUE_HEADS * HEAD_SIZE), 1.0, 6.0, ((0, 256),))
    output_gradient = gaussian(key_of[3], (TOTAL_ROWS, QUERY_HEADS * HEAD_SIZE), 1.0, 6.0, ((0, 256),))
    document_lengths = draw_document_lengths(jax.random.fold_in(key_of[5], 71), 0)
    return dict(query_input=query_input, key_input=key_input, value_input=value_input, output_gradient=output_gradient, document_lengths=document_lengths)


NEGATIVE = -1e+30

def document_index(lengths, positions):
    doc_ends = jnp.cumsum(lengths).astype(jnp.int32)
    return lax.optimization_barrier(jnp.sum((positions[:, None] >= doc_ends[None, :]).astype(jnp.int32), axis=1))

def rounded(values):
    lowered = lax.optimization_barrier(values.astype(jnp.bfloat16))
    return lowered.astype(jnp.float32)

def group_pass(pieces, allowed, blocks):
    query_rows, current_keys, current_values, current_gradients = pieces
    scaling = 1.0 / math.sqrt(HEAD_SIZE)
    heads, rows_per_pack, head_dim = query_rows.shape
    query_wide = query_rows.astype(jnp.float32)
    key_wide = current_keys.astype(jnp.float32)
    value_wide = current_values.astype(jnp.float32)
    grad_wide = current_gradients.astype(jnp.float32)
    scores = jnp.einsum('gqd,kd->gqk', query_wide, key_wide) * scaling
    scores = jnp.where(allowed[None, :, :], scores, NEGATIVE)
    row_max = lax.optimization_barrier(jnp.max(scores, axis=-1, keepdims=True))
    weights = jnp.exp(scores - row_max)
    attn_probs = weights / lax.optimization_barrier(jnp.sum(weights, axis=-1, keepdims=True))
    probs_low = rounded(attn_probs)
    attention_fn = rounded(jnp.einsum('gqk,kd->gqd', probs_low, value_wide))
    dprobs = jnp.einsum('gqd,kd->gqk', grad_wide, value_wide)
    row_delta = lax.optimization_barrier(jnp.sum(grad_wide * attention_fn, axis=-1, keepdims=True))
    dscore = rounded(attn_probs * (dprobs - row_delta))
    query_gradient = jnp.einsum('gqk,kd->gqd', dscore, key_wide) * scaling
    block_rows = rows_per_pack // blocks
    dscore_blocks = dscore.reshape(heads, blocks, block_rows, rows_per_pack)
    query_blocks = query_wide.reshape(heads, blocks, block_rows, head_dim)
    probs_blocks = probs_low.reshape(heads, blocks, block_rows, rows_per_pack)
    grad_blocks = grad_wide.reshape(heads, blocks, block_rows, head_dim)
    key_terms = rounded(jnp.einsum('gtqk,gtqd->tkd', dscore_blocks, query_blocks) * scaling)
    value_terms = rounded(jnp.einsum('gtqk,gtqd->tkd', probs_blocks, grad_blocks))
    return (attention_fn.astype(jnp.bfloat16), query_gradient.astype(jnp.bfloat16), lax.optimization_barrier(jnp.sum(key_terms, axis=0)).astype(jnp.bfloat16), lax.optimization_barrier(jnp.sum(value_terms, axis=0)).astype(jnp.bfloat16))

def one_pack(inputs):
    query_rows, current_keys, current_values, current_gradients, lengths = inputs
    rows_per_pack = query_rows.shape[0]
    repeat_count = QUERY_HEADS // KEY_VALUE_HEADS
    positions = jnp.arange(rows_per_pack, dtype=jnp.int32)
    segment = document_index(lengths, positions)
    allowed = (segment[:, None] == segment[None, :]) & (positions[None, :] <= positions[:, None])
    grouped_queries = query_rows.reshape(rows_per_pack, KEY_VALUE_HEADS, repeat_count, HEAD_SIZE).transpose(1, 2, 0, 3)
    grouped_gradient = current_gradients.reshape(rows_per_pack, KEY_VALUE_HEADS, repeat_count, HEAD_SIZE).transpose(1, 2, 0, 3)
    grouped_keys = current_keys.reshape(rows_per_pack, KEY_VALUE_HEADS, HEAD_SIZE).transpose(1, 0, 2)
    grouped_values = current_values.reshape(rows_per_pack, KEY_VALUE_HEADS, HEAD_SIZE).transpose(1, 0, 2)
    attention_fn, query_gradient, key_gradient, value_gradient = lax.map(lambda pieces: group_pass(pieces, allowed, N_TENSOR), (grouped_queries, grouped_keys, grouped_values, grouped_gradient))
    attention_fn = attention_fn.transpose(2, 0, 1, 3).reshape(rows_per_pack, QUERY_HEADS * HEAD_SIZE)
    query_gradient = query_gradient.transpose(2, 0, 1, 3).reshape(rows_per_pack, QUERY_HEADS * HEAD_SIZE)
    key_gradient = key_gradient.transpose(1, 0, 2).reshape(rows_per_pack, KEY_VALUE_HEADS * HEAD_SIZE)
    value_gradient = value_gradient.transpose(1, 0, 2).reshape(rows_per_pack, KEY_VALUE_HEADS * HEAD_SIZE)
    return (attention_fn, query_gradient, key_gradient, value_gradient)

def reference(query_input, key_input, value_input, output_gradient, document_lengths):
    pack_count = document_lengths.shape[0]
    rows_per_pack = query_input.shape[0] // pack_count
    reshaped_rows = (query_input.reshape(pack_count, rows_per_pack, QUERY_HEADS * HEAD_SIZE), key_input.reshape(pack_count, rows_per_pack, KEY_VALUE_HEADS * HEAD_SIZE), value_input.reshape(pack_count, rows_per_pack, KEY_VALUE_HEADS * HEAD_SIZE), output_gradient.reshape(pack_count, rows_per_pack, QUERY_HEADS * HEAD_SIZE), document_lengths)
    attention_fn, query_gradient, key_gradient, value_gradient = lax.map(one_pack, reshaped_rows)
    return (attention_fn.reshape(pack_count * rows_per_pack, QUERY_HEADS * HEAD_SIZE), query_gradient.reshape(pack_count * rows_per_pack, QUERY_HEADS * HEAD_SIZE), key_gradient.reshape(pack_count * rows_per_pack, KEY_VALUE_HEADS * HEAD_SIZE), value_gradient.reshape(pack_count * rows_per_pack, KEY_VALUE_HEADS * HEAD_SIZE))
```

```python
import math

import jax
import jax.numpy as jnp
from jax import lax
from jax.experimental import pallas as pl
from jax.experimental.pallas import tpu as pltpu
from jax.sharding import PartitionSpec as P

GROUPS = 8
REPEAT = 8
DEPTH = 128
ROWS = 128
RING = 8
PACK = ROWS * RING
WIDE = REPEAT * DEPTH
DOCS = 8
NEGATIVE = -1e30
SCALE = 1.0 / math.sqrt(DEPTH)
EXP2_SCALE = SCALE * math.log2(math.e)

UP = (4, 4, 4, 3, 3, 2, 1, 0)
DOWN = (3, 3, 3, 4, 0, 0, 0, 0)
HOPS = 4
TICKS = GROUPS + 2 * HOPS

MESH = pl.DeviceIdType.MESH
F32 = jnp.float32
BF16 = jnp.bfloat16


def product(a, b, left, right):
    return lax.dot_general(a, b, (((left,), (right,)), ((), ())), preferred_element_type=F32)


def kernel(
    query_hbm, key_hbm, value_hbm, grad_hbm, lengths,
    out_hbm, dquery_hbm, dkey_hbm, dvalue_hbm,
    query, grad, out, dquery, kv, terms, partial, second, bias, dkv,
    kv_in, up_out, down_out, part_in, second_in, part_out, load_sem, own_sem, store_sem, final_sem,
):
    dp = lax.axis_index("dp")
    z = lax.axis_index("tensor")
    above = lax.rem(z + 1, RING)
    below = lax.rem(z + RING - 1, RING)

    def columns(g, width):
        return pl.ds(pl.multiple_of(g * width, width), width)

    def own_copy(g, which):
        source = (key_hbm, value_hbm)[which]
        return pltpu.make_async_copy(
            source.at[:, columns(g, DEPTH)], kv.at[g, z, which], own_sem.at[g, which]
        )

    load_query = pltpu.make_async_copy(query_hbm, query, load_sem.at[0])
    load_grad = pltpu.make_async_copy(grad_hbm, grad, load_sem.at[1])

    for g in range(GROUPS):
        own_copy(g, 0).start()
        own_copy(g, 1).start()
    load_query.start()
    load_grad.start()

    barrier = pltpu.get_barrier_semaphore()
    for neighbour in (above, below):
        pl.semaphore_signal(barrier, inc=1, device_id=(dp, neighbour), device_id_type=MESH)

    for b in range(HOPS, RING):
        @pl.when(z < b)
        def _(b=b):
            for g in range(GROUPS):
                kv[g, b] = jnp.zeros((2, ROWS, DEPTH), BF16)

    row_pos = z * ROWS + lax.broadcasted_iota(jnp.int32, (ROWS, PACK), 0)
    col_pos = lax.broadcasted_iota(jnp.int32, (ROWS, PACK), 1)
    row_doc = jnp.zeros((ROWS, PACK), jnp.int32)
    col_doc = jnp.zeros((ROWS, PACK), jnp.int32)
    end = jnp.int32(0)
    for k in range(DOCS):
        end = end + lengths[dp, k]
        row_doc = row_doc + (row_pos >= end).astype(jnp.int32)
        col_doc = col_doc + (col_pos >= end).astype(jnp.int32)
    bias[...] = jnp.where((row_doc == col_doc) & (col_pos <= row_pos), 0.0, NEGATIVE)

    pl.semaphore_wait(barrier, 2)

    def send_up(g, b):
        return pltpu.make_async_remote_copy(
            src_ref=kv.at[g, b], dst_ref=kv.at[g, b], send_sem=up_out.at[g, b],
            recv_sem=kv_in.at[g, b], device_id=(dp, above), device_id_type=MESH,
        )

    def send_down(g, b):
        return pltpu.make_async_remote_copy(
            src_ref=kv.at[g, b], dst_ref=kv.at[g, b], send_sem=down_out.at[g, b],
            recv_sem=kv_in.at[g, b], device_id=(dp, below), device_id_type=MESH,
        )

    def from_below(hop):
        return z - hop, (z >= hop) & ((z < RING - 1) | (hop < 4))

    def goes_up(hop):
        return (z >= hop) & (z < RING - 1) & (hop < 4) & ((z < RING - 2) | (hop < 3))

    def from_above(hop):
        b = lax.rem(z + hop, RING)
        return b, (b <= 3) & ((b == 3) | (hop <= 3))

    def goes_down(hop):
        b = lax.rem(z + hop, RING)
        return (b <= 3) & (hop < 4) & ((b == 3) | (hop < 3))

    def gather_step(g, hop):
        b, comes = from_below(hop)

        @pl.when(comes)
        def _():
            send_up(g, b).wait_recv()

        @pl.when(goes_up(hop))
        def _():
            send_up(g, b).start()

        c, falls = from_above(hop)

        @pl.when(falls)
        def _():
            send_down(g, c).wait_recv()

        @pl.when(goes_down(hop))
        def _():
            send_down(g, c).start()

    def gather_sent(g):
        for hop in range(HOPS):
            @pl.when(goes_up(hop))
            def _(hop=hop):
                send_up(g, z - hop).wait_send()

            @pl.when(goes_down(hop))
            def _(hop=hop):
                send_down(g, lax.rem(z + hop, RING)).wait_send()

    def pass_down(source, g, b):
        return pltpu.make_async_remote_copy(
            src_ref=source.at[g, b], dst_ref=partial.at[g, b], send_sem=part_out.at[g, b],
            recv_sem=part_in.at[g, b], device_id=(dp, below), device_id_type=MESH,
        )

    def pass_up(source, g, b, last):
        return pltpu.make_async_remote_copy(
            src_ref=source.at[g, b],
            dst_ref=second.at[g] if last else partial.at[g, b],
            send_sem=part_out.at[g, b],
            recv_sem=second_in.at[g] if last else part_in.at[g, b],
            device_id=(dp, above), device_id_type=MESH,
        )

    def add_own(g, b):
        total = partial[g, b].astype(F32) + terms[g, b].astype(F32)
        partial[g, b] = total.astype(BF16)

    def return_step(g, phase):
        for b in range(RING):
            distance = UP[b] - phase
            if UP[b] and distance > 0:
                @pl.when(z == b + distance)
                def _(b=b):
                    if phase:
                        pass_down(partial, g, b).wait_recv()
                        add_own(g, b)
                        pass_down(partial, g, b).start()
                    else:
                        pass_down(terms, g, b).start()
            distance = DOWN[b] - phase
            if DOWN[b] and distance > 0:
                place = (b - distance) % RING

                @pl.when(z == place)
                def _(b=b, distance=distance, place=place):
                    if phase:
                        pass_up(partial, g, b, False).wait_recv()
                        if place > b:
                            add_own(g, b)
                        pass_up(partial, g, b, distance == 1).start()
                    else:
                        pass_up(terms, g, b, distance == 1).start()

    def return_end(g):
        dkv[...] = terms[g, z].astype(F32)

        @pl.when(z < RING - 1)
        def _():
            pass_down(partial, g, z).wait_recv()
            dkv[...] += partial[g, z].astype(F32)

        @pl.when(z < 4)
        def _():
            pass_up(partial, g, z, True).wait_recv()
            dkv[...] += second[g].astype(F32)

        terms[g, z] = dkv[...].astype(BF16)
        final_copy(g, 0).start()
        final_copy(g, 1).start()

    def final_copy(g, which):
        target = (dkey_hbm, dvalue_hbm)[which]
        return pltpu.make_async_copy(
            terms.at[g, z, which], target.at[:, columns(g, DEPTH)], final_sem.at[g, which]
        )

    def return_sent(g):
        for b in range(RING):
            if UP[b]:
                @pl.when((z > b) & (z <= b + UP[b]))
                def _(b=b):
                    pass_down(partial, g, b).wait_send()
            if DOWN[b]:
                away = lax.rem(b - z + RING, RING)

                @pl.when((away > 0) & (away <= DOWN[b]))
                def _(b=b):
                    pass_up(partial, g, b, False).wait_send()

    def store_copy(g, which):
        source, target = ((out, out_hbm), (dquery, dquery_hbm))[which]
        return pltpu.make_async_copy(
            source.at[:, columns(g, WIDE)], target.at[:, columns(g, WIDE)], store_sem.at[g, which]
        )

    def attend(g):
        keys = kv[g, :, 0].reshape(PACK, DEPTH)
        values = kv[g, :, 1].reshape(PACK, DEPTH)
        heads = [columns(g * REPEAT + h, DEPTH) for h in range(REPEAT)]
        queries = jnp.concatenate([query[:, c] for c in heads], axis=0)
        grads = jnp.concatenate([grad[:, c] for c in heads], axis=0)
        scores = product(queries, keys, 1, 1) + jnp.concatenate([bias[...]] * REPEAT, axis=0)
        row_max = jnp.max(scores, axis=1, keepdims=True)
        weights = jnp.exp2((scores - row_max) * EXP2_SCALE).astype(BF16)
        values_ones = jnp.concatenate([values, jnp.ones((PACK, DEPTH), BF16)], axis=1)
        summed = product(weights, values_ones, 1, 0)
        inverse = 1.0 / summed[:, DEPTH:]
        attn_out = (summed[:, :DEPTH] * inverse).astype(BF16)
        grads = (grads.astype(F32) * inverse).astype(BF16)
        delta = jnp.sum(grads.astype(F32) * attn_out.astype(F32), axis=1, keepdims=True)
        dprobs = product(grads, values, 1, 1)
        dscore = (dprobs - delta).astype(BF16) * weights
        dqueries = (product(dscore, keys, 1, 0) * SCALE).astype(BF16)
        for h, c in enumerate(heads):
            out[:, c] = attn_out[h * ROWS:(h + 1) * ROWS]
            dquery[:, c] = dqueries[h * ROWS:(h + 1) * ROWS]
        store_copy(g, 0).start()
        store_copy(g, 1).start()
        key_terms = (product(dscore, queries, 0, 0) * SCALE).astype(BF16)
        value_terms = product(weights, grads, 0, 0).astype(BF16)
        terms[g, :, 0] = key_terms.reshape(RING, ROWS, DEPTH)
        terms[g, :, 1] = value_terms.reshape(RING, ROWS, DEPTH)

    def in_range(g):
        return (g >= 0) & (g < GROUPS)

    def tick(t, _):
        for hop in range(HOPS, -1, -1):
            @pl.when(in_range(t - hop))
            def _(hop=hop):
                if hop == 0:
                    own_copy(t, 0).wait()
                    own_copy(t, 1).wait()
                gather_step_any(t - hop, hop)

        g = t - HOPS

        @pl.when(t == HOPS)
        def _():
            load_query.wait()
            load_grad.wait()

        @pl.when(in_range(g))
        def _():
            attend(g)

        for phase in range(HOPS, -1, -1):
            @pl.when(in_range(g - phase))
            def _(phase=phase):
                if phase == HOPS:
                    return_end(g - phase)
                else:
                    return_step(g - phase, phase)

        return 0

    def gather_step_any(g, hop):
        if hop:
            gather_step(g, hop)
        else:
            @pl.when(goes_up(0))
            def _():
                send_up(g, z).start()

            @pl.when(goes_down(0))
            def _():
                send_down(g, z).start()

    lax.fori_loop(0, TICKS, tick, 0)

    def finish(g, _):
        gather_sent(g)
        return_sent(g)
        for which in range(2):
            store_copy(g, which).wait()
            final_copy(g, which).wait()
        return 0

    lax.fori_loop(0, GROUPS, finish, 0)


def body(query_input, key_input, value_input, output_gradient, document_lengths):
    anywhere = pl.BlockSpec(memory_space=pl.ANY)
    wide = jax.ShapeDtypeStruct((ROWS, GROUPS * WIDE), BF16)
    narrow = jax.ShapeDtypeStruct((ROWS, GROUPS * DEPTH), BF16)
    rows = pltpu.VMEM((ROWS, GROUPS * WIDE), BF16)
    blocks = pltpu.VMEM((GROUPS, RING, 2, ROWS, DEPTH), BF16)
    sems = pltpu.SemaphoreType.DMA
    return pl.pallas_call(
        kernel,
        out_shape=(wide, wide, narrow, narrow),
        in_specs=[anywhere] * 4 + [pl.BlockSpec(memory_space=pltpu.SMEM)],
        out_specs=(anywhere,) * 4,
        scratch_shapes=[
            rows, rows, rows, rows,
            blocks, blocks, blocks,
            pltpu.VMEM((GROUPS, 2, ROWS, DEPTH), BF16),
            pltpu.VMEM((ROWS, PACK), F32),
            pltpu.VMEM((2, ROWS, DEPTH), F32),
            sems((GROUPS, RING)), sems((GROUPS, RING)), sems((GROUPS, RING)),
            sems((GROUPS, RING)), sems((GROUPS,)), sems((GROUPS, RING)),
            sems((2,)), sems((GROUPS, 2)), sems((GROUPS, 2)), sems((GROUPS, 2)),
        ],
        compiler_params=pltpu.CompilerParams(
            collective_id=0, has_side_effects=True, vmem_limit_bytes=56 * 2**20
        ),
    )(query_input, key_input, value_input, output_gradient, document_lengths)


def solution(mesh):
    rows = P(("dp", "tensor"), None)
    return jax.shard_map(
        body,
        mesh=mesh,
        in_specs=(rows, rows, rows, rows, P()),
        out_specs=(rows, rows, rows, rows),
        check_vma=False,
    )
```

```python
import math

import jax
import jax.numpy as jnp
from jax import lax
from jax.experimental import pallas as pl
from jax.experimental.pallas import tpu as pltpu
from jax.sharding import PartitionSpec as P

GROUPS = 8
REPEAT = 8
DEPTH = 128
ROWS = 128
RING = 8
PACK = ROWS * RING
WIDE = REPEAT * DEPTH
DOCS = 8
PACKS = 32
NEGATIVE = -1e30
SCALE = 1.0 / math.sqrt(DEPTH)
EXP2_SCALE = SCALE * math.log2(math.e)

STREAMS = 1
UP = ((4, 4, 4, 3, 3, 2, 1, 0),)
DOWN = ((3, 3, 3, 4, 0, 0, 0, 0),)

OWN_UP, OWN_DOWN, FROM_BELOW, FROM_ABOVE, END_UP, END_DOWN, BACK_DOWN, BACK_UP, FINAL = range(9)
PARTS = 1
FIRST_TICK = -7
LAST_TICK = GROUPS - 1 + 7
PLAN = (
    (
        ((7, 1, 5), (3, 2, -1), (8, 0, 7), (7, 2, 3), (3, 1, -2), (3, 3, -1), (7, 3, 2), (1, 0, -7),
         (0, 0, -7),),
    ),
    (
        ((7, 2, 4), (3, 2, -4), (7, 3, 2), (3, 3, -4), (6, 0, 4), (1, 1, -6), (8, 1, 5), (0, 1, -7),
         (2, 0, -5),),
    ),
    (
        ((6, 0, 2), (6, 1, 3), (0, 2, -5), (2, 0, -3), (1, 2, -5), (7, 3, 3), (2, 1, -5), (8, 2, 5),
         (3, 3, -5),),
    ),
    (
        ((1, 3, -6), (2, 0, -2), (8, 3, 7), (0, 3, -6), (6, 0, 1), (6, 1, 2), (6, 2, 3), (2, 2, -4),
         (2, 1, -4),),
    ),
    (
        ((2, 2, -2), (4, 0, 0), (2, 1, -2), (6, 2, 2), (0, 4, -6), (8, 4, 5), (2, 3, -4), (6, 3, 3),
         (6, 1, 0), (2, 0, -1),),
    ),
    (
        ((4, 1, 0), (2, 2, -1), (6, 3, 2), (2, 4, -3), (5, 0, 1), (2, 3, -2), (0, 5, -7), (6, 2, 1),
         (6, 4, 3), (8, 5, 7), (3, 0, -2), (2, 1, -1),),
    ),
    (
        ((4, 2, 0), (4, 3, 0), (2, 4, -2), (0, 6, -6), (7, 0, 2), (3, 0, -5), (3, 1, -1), (6, 4, 1),
         (2, 3, -1), (8, 6, 5), (5, 1, 0), (6, 5, 3), (2, 5, -3), (2, 2, -1),),
    ),
    (
        ((4, 4, 0), (5, 3, 0), (3, 1, -2), (3, 0, -6), (2, 6, -2), (7, 0, 3), (5, 2, 0), (4, 5, 0),
         (4, 6, 1), (2, 5, -1), (3, 2, -1), (2, 4, -1), (3, 3, -1), (7, 1, 1), (8, 7, 0),),
    ),
)

MESH = pl.DeviceIdType.MESH
F32 = jnp.float32
BF16 = jnp.bfloat16


def product(a, b, left, right):
    return lax.dot_general(a, b, (((left,), (right,)), ((), ())), preferred_element_type=F32)


def kernel(
    query_hbm, key_hbm, value_hbm, grad_hbm, lengths_hbm,
    out, dquery, dkv_out,
    lengths, query, grad, kv, terms, partial, second, bias, dkv,
    kv_in, up_out, down_out, part_in, second_in, part_out, load_sem, own_sem,
):
    dp = lax.axis_index("dp")
    z = lax.axis_index("tensor")
    above = lax.rem(z + 1, RING)
    below = lax.rem(z + RING - 1, RING)

    def columns(g, width):
        return pl.ds(pl.multiple_of(g * width, width), width)

    def own_copy(g, which):
        source = (key_hbm, value_hbm)[which]
        return pltpu.make_async_copy(
            source.at[:, columns(g, DEPTH)], kv.at[g, z, which], own_sem.at[g, which]
        )

    load_query = pltpu.make_async_copy(query_hbm, query, load_sem.at[0])
    load_grad = pltpu.make_async_copy(grad_hbm, grad, load_sem.at[1])
    load_lengths = pltpu.make_async_copy(lengths_hbm, lengths, load_sem.at[2])

    barrier = pltpu.get_barrier_semaphore()
    for neighbour in (above, below):
        pl.semaphore_signal(barrier, inc=1, device_id=(dp, neighbour), device_id_type=MESH)

    load_lengths.start()
    for g in range(GROUPS):
        own_copy(g, 0).start()
        own_copy(g, 1).start()
    load_query.start()
    load_grad.start()

    def piece(s):
        return (s,) if STREAMS > 1 else ()

    for s in range(STREAMS):
        for b in range(1, RING):
            if not DOWN[s][b]:
                @pl.when(z < b)
                def _(b=b, s=s):
                    for g in range(GROUPS):
                        at = (g, b) + piece(s)
                        kv[at] = jnp.zeros(kv.at[at].shape, BF16)

    load_lengths.wait()
    row_pos = z * ROWS + lax.broadcasted_iota(jnp.int32, (PACK, ROWS), 1)
    col_pos = lax.broadcasted_iota(jnp.int32, (PACK, ROWS), 0)
    row_doc = jnp.zeros((PACK, ROWS), jnp.int32)
    col_doc = jnp.zeros((PACK, ROWS), jnp.int32)
    end = jnp.int32(0)
    for k in range(DOCS):
        end = end + lengths[k, dp]
        row_doc = row_doc + (row_pos >= end).astype(jnp.int32)
        col_doc = col_doc + (col_pos >= end).astype(jnp.int32)
    bias[...] = jnp.where((row_doc == col_doc) & (col_pos <= row_pos), 0.0, NEGATIVE)

    def forward(g, b, s, up):
        here = kv.at[(g, b) + piece(s)]
        return pltpu.make_async_remote_copy(
            src_ref=here, dst_ref=here, send_sem=(up_out if up else down_out).at[g, b, s],
            recv_sem=kv_in.at[g, b, s], device_id=(dp, above if up else below), device_id_type=MESH,
        )

    def back(source, g, b, s, up, last=False):
        at = (g, b) + piece(s)
        return pltpu.make_async_remote_copy(
            src_ref=source.at[at],
            dst_ref=second.at[(g,) + piece(s)] if last else partial.at[at],
            send_sem=part_out.at[g, b, s],
            recv_sem=second_in.at[g, s] if last else part_in.at[g, b, s],
            device_id=(dp, above if up else below), device_id_type=MESH,
        )

    def add_own(g, b, s):
        at = (g, b) + piece(s)
        partial[at] = (partial[at].astype(F32) + terms[at].astype(F32)).astype(BF16)

    def step(kind, place, b, s, g):
        if kind == OWN_UP:
            forward(g, b, s, True).start()
        elif kind == OWN_DOWN:
            forward(g, b, s, False).start()
        elif kind == FROM_BELOW:
            forward(g, b, s, True).wait_recv()
            if place - b < UP[s][b]:
                forward(g, b, s, True).start()
        elif kind == FROM_ABOVE:
            forward(g, b, s, False).wait_recv()
            if (b - place) % RING < DOWN[s][b]:
                forward(g, b, s, False).start()
        elif kind == END_UP:
            back(terms, g, b, s, False).start()
        elif kind == END_DOWN:
            back(terms, g, b, s, True, (b - place) % RING == 1).start()
        elif kind == BACK_DOWN:
            back(partial, g, b, s, False).wait_recv()
            add_own(g, b, s)
            back(partial, g, b, s, False).start()
        elif kind == BACK_UP:
            back(partial, g, b, s, True).wait_recv()
            if place > b:
                add_own(g, b, s)
            back(partial, g, b, s, True, (b - place) % RING == 1).start()
        else:
            at = (g, b) + piece(s)
            total = terms[at].astype(F32)
            if UP[s][b]:
                back(partial, g, b, s, False).wait_recv()
                total = total + partial[at].astype(F32)
            if DOWN[s][b]:
                back(partial, g, b, s, True, True).wait_recv()
                total = total + second[(g,) + piece(s)].astype(F32)
            dkv_out[(g,) + piece(s)] = total.astype(BF16)

    def sent(g):
        for place in range(RING):
            @pl.when(z == place)
            def _(place=place):
                for entry in [entry for part in PLAN[place] for entry in part]:
                    kind, b = entry[:2]
                    s = entry[3] if STREAMS > 1 else 0
                    if kind == OWN_UP or (kind == FROM_BELOW and place - b < UP[s][b]):
                        forward(g, b, s, True).wait_send()
                    elif kind == OWN_DOWN or (
                        kind == FROM_ABOVE and (b - place) % RING < DOWN[s][b]
                    ):
                        forward(g, b, s, False).wait_send()
                    elif kind in (END_UP, BACK_DOWN, END_DOWN, BACK_UP):
                        back(partial, g, b, s, kind in (END_DOWN, BACK_UP)).wait_send()

    def attend(g, part):
        keys = kv[g, :, 0].reshape(PACK, DEPTH)
        values = kv[g, :, 1].reshape(PACK, DEPTH)
        count = REPEAT // PARTS
        heads = [columns(g * REPEAT + part * count + h, DEPTH) for h in range(count)]
        queries = jnp.concatenate([query[:, c] for c in heads], axis=0)
        grads = jnp.concatenate([grad[:, c] for c in heads], axis=0)
        scores = product(keys, queries, 1, 1) + jnp.concatenate([bias[...]] * count, axis=1)
        row_max = jnp.max(scores, axis=0, keepdims=True)
        raised = jnp.exp2((scores - row_max) * EXP2_SCALE)
        inverse = 1.0 / jnp.sum(raised, axis=0, keepdims=True)
        weights = raised.astype(BF16)
        attn_out = (product(values, weights, 0, 0) * inverse).T.astype(BF16)
        grads = (grads.astype(F32) * jnp.broadcast_to(inverse, (DEPTH, count * ROWS)).T).astype(BF16)
        delta = jnp.sum(grads.astype(F32) * attn_out.astype(F32), axis=1, keepdims=True)
        delta = jnp.broadcast_to(delta, (count * ROWS, DEPTH)).T[:1]
        dscore = (product(values, grads, 1, 1) - delta).astype(BF16) * weights
        dqueries = (product(keys, dscore, 0, 0).T * SCALE).astype(BF16)
        for h, c in enumerate(heads):
            out[:, c] = attn_out[h * ROWS:(h + 1) * ROWS]
            dquery[:, c] = dqueries[h * ROWS:(h + 1) * ROWS]
        key_terms = product(dscore, queries, 1, 0)
        value_terms = product(weights, grads, 1, 0)
        if part:
            key_terms = key_terms + dkv[0]
            value_terms = value_terms + dkv[1]
        if part < PARTS - 1:
            dkv[0] = key_terms
            dkv[1] = value_terms
        else:
            terms[g, :, 0] = (key_terms * SCALE).astype(BF16).reshape(RING, ROWS, DEPTH)
            terms[g, :, 1] = value_terms.astype(BF16).reshape(RING, ROWS, DEPTH)

    def in_range(g):
        return (g >= 0) & (g < GROUPS)

    def tick(index, _):
        t = index + FIRST_TICK

        @pl.when(t == 0)
        def _():
            load_query.wait()
            load_grad.wait()

        for part in range(PARTS):
            @pl.when(in_range(t))
            def _(part=part):
                attend(t, part)

            for place in range(RING):
                @pl.when(z == place)
                def _(part=part, place=place):
                    for entry in PLAN[place][part]:
                        kind, b, offset = entry[:3]

                        @pl.when(in_range(t - offset))
                        def _(entry=entry, kind=kind, b=b, offset=offset):
                            step(kind, place, b, entry[3] if STREAMS > 1 else 0, t - offset)

        return 0

    for g in range(GROUPS):
        own_copy(g, 0).wait()
        own_copy(g, 1).wait()
    pl.semaphore_wait(barrier, 2)

    lax.fori_loop(0, LAST_TICK + 1 - FIRST_TICK, tick, 0)

    def finish(g, _):
        sent(g)
        return 0

    lax.fori_loop(0, GROUPS, finish, 0)


def store(out, dquery, dkv, out_hbm, dquery_hbm, dkey_hbm, dvalue_hbm, sem):
    copies = [
        pltpu.make_async_copy(out, out_hbm, sem.at[0]),
        pltpu.make_async_copy(dquery, dquery_hbm, sem.at[1]),
    ]
    for g in range(GROUPS):
        place = pl.ds(g * DEPTH, DEPTH)
        for which, target in enumerate((dkey_hbm, dvalue_hbm)):
            copies.append(pltpu.make_async_copy(
                dkv.at[g, which], target.at[:, place], sem.at[2 + 2 * g + which]
            ))
    for copy in copies:
        copy.start()
    for copy in copies:
        copy.wait()


def body(query_input, key_input, value_input, output_gradient, document_lengths):
    hbm = pl.BlockSpec(memory_space=pltpu.HBM)
    wide = jax.ShapeDtypeStruct((ROWS, GROUPS * WIDE), BF16)
    narrow = jax.ShapeDtypeStruct((ROWS, GROUPS * DEPTH), BF16)
    rows = pltpu.VMEM((ROWS, GROUPS * WIDE), BF16)
    blocks = pltpu.VMEM((GROUPS, RING, 2, ROWS, DEPTH), BF16)
    gathered = pltpu.VMEM((GROUPS, 2, ROWS, DEPTH), BF16)
    sems = pltpu.SemaphoreType.DMA
    each = sems((GROUPS, RING, STREAMS))
    inputs = [
        pltpu.with_memory_space_constraint(x, pltpu.HBM)
        for x in (query_input, key_input, value_input, output_gradient, document_lengths.T)
    ]
    held = pl.pallas_call(
        kernel,
        out_shape=(rows, rows, gathered),
        in_specs=[hbm] * 5,
        out_specs=(pl.BlockSpec(memory_space=pltpu.VMEM),) * 3,
        scratch_shapes=[
            pltpu.SMEM((DOCS, PACKS), jnp.int32),
            rows, rows,
            blocks, blocks, blocks, gathered,
            pltpu.VMEM((PACK, ROWS), F32),
            pltpu.VMEM((2, PACK, DEPTH), F32),
            each, each, each, each, sems((GROUPS, STREAMS)), each,
            sems((3,)), sems((GROUPS, 2)),
        ],
        compiler_params=pltpu.CompilerParams(
            collective_id=0, has_side_effects=True, vmem_limit_bytes=48 * 2**20
        ),
    )(*inputs)
    return pl.pallas_call(
        store,
        out_shape=(wide, wide, narrow, narrow),
        in_specs=[pl.BlockSpec(memory_space=pl.ANY)] * 3,
        out_specs=(hbm,) * 4,
        scratch_shapes=[sems((2 + 2 * GROUPS,))],
        compiler_params=pltpu.CompilerParams(vmem_limit_bytes=2**20),
    )(*held)


def solution(mesh):
    rows = P(("dp", "tensor"), None)
    return jax.shard_map(
        body,
        mesh=mesh,
        in_specs=(rows, rows, rows, rows, P()),
        out_specs=(rows, rows, rows, rows),
        check_vma=False,
    )
```

```python
import math

import jax
import jax.numpy as jnp
from jax import lax
from jax.experimental import pallas as pl
from jax.experimental.pallas import tpu as pltpu
from jax.sharding import PartitionSpec as P

GROUPS = 8
REPEAT = 8
DEPTH = 128
ROWS = 128
RING = 8
PACK = ROWS * RING
WIDE = REPEAT * DEPTH
DOCS = 8
PACKS = 32
NEGATIVE = -1e30
SCALE = 1.0 / math.sqrt(DEPTH)
EXP2_SCALE = SCALE * math.log2(math.e)

STREAMS = 1
UP = ((4, 4, 4, 3, 3, 2, 1, 0),)
DOWN = ((3, 3, 3, 4, 0, 0, 0, 0),)

OWN_UP, OWN_DOWN, FROM_BELOW, FROM_ABOVE, END_UP, END_DOWN, BACK_DOWN, BACK_UP, FINAL = range(9)
PARTS = 1
FIRST_TICK = -7
LAST_TICK = GROUPS - 1 + 7
PLAN = (
    (
        ((7, 1, 5), (3, 2, -1), (8, 0, 7), (7, 2, 3), (3, 1, -2), (3, 3, -1), (7, 3, 2), (1, 0, -7),
         (0, 0, -7),),
    ),
    (
        ((7, 2, 4), (3, 2, -4), (7, 3, 2), (3, 3, -4), (6, 0, 4), (1, 1, -6), (8, 1, 5), (0, 1, -7),
         (2, 0, -5),),
    ),
    (
        ((6, 0, 2), (6, 1, 3), (0, 2, -5), (2, 0, -3), (1, 2, -5), (7, 3, 3), (2, 1, -5), (8, 2, 5),
         (3, 3, -5),),
    ),
    (
        ((1, 3, -6), (2, 0, -2), (8, 3, 7), (0, 3, -6), (6, 0, 1), (6, 1, 2), (6, 2, 3), (2, 2, -4),
         (2, 1, -4),),
    ),
    (
        ((2, 2, -2), (4, 0, 0), (2, 1, -2), (6, 2, 2), (0, 4, -6), (8, 4, 5), (2, 3, -4), (6, 3, 3),
         (6, 1, 0), (2, 0, -1),),
    ),
    (
        ((4, 1, 0), (2, 2, -1), (6, 3, 2), (2, 4, -3), (5, 0, 1), (2, 3, -2), (0, 5, -7), (6, 2, 1),
         (6, 4, 3), (8, 5, 7), (3, 0, -2), (2, 1, -1),),
    ),
    (
        ((4, 2, 0), (4, 3, 0), (2, 4, -2), (0, 6, -6), (7, 0, 2), (3, 0, -5), (3, 1, -1), (6, 4, 1),
         (2, 3, -1), (8, 6, 5), (5, 1, 0), (6, 5, 3), (2, 5, -3), (2, 2, -1),),
    ),
    (
        ((4, 4, 0), (5, 3, 0), (3, 1, -2), (3, 0, -6), (2, 6, -2), (7, 0, 3), (5, 2, 0), (4, 5, 0),
         (4, 6, 1), (2, 5, -1), (3, 2, -1), (2, 4, -1), (3, 3, -1), (7, 1, 1), (8, 7, 0),),
    ),
)

MESH = pl.DeviceIdType.MESH
F32 = jnp.float32
BF16 = jnp.bfloat16


def product(a, b, left, right):
    return lax.dot_general(a, b, (((left,), (right,)), ((), ())), preferred_element_type=F32)


def kernel(
    query_hbm, key_hbm, value_hbm, grad_hbm, lengths_hbm,
    out, dquery, dkv_out,
    lengths, query, grad, kv, terms, partial, second, bias, dkv,
    kv_in, up_out, down_out, part_in, second_in, part_out, load_sem, own_sem,
):
    dp = lax.axis_index("dp")
    z = lax.axis_index("tensor")
    above = lax.rem(z + 1, RING)
    below = lax.rem(z + RING - 1, RING)

    def columns(g, width):
        return pl.ds(pl.multiple_of(g * width, width), width)

    def own_copy(g, which):
        source = (key_hbm, value_hbm)[which]
        return pltpu.make_async_copy(
            source.at[:, columns(g, DEPTH)], kv.at[g, z, which], own_sem.at[g, which]
        )

    load_query = pltpu.make_async_copy(query_hbm, query, load_sem.at[0])
    load_grad = pltpu.make_async_copy(grad_hbm, grad, load_sem.at[1])
    load_lengths = pltpu.make_async_copy(lengths_hbm, lengths, load_sem.at[2])

    barrier = pltpu.get_barrier_semaphore()
    for neighbour in (above, below):
        pl.semaphore_signal(barrier, inc=1, device_id=(dp, neighbour), device_id_type=MESH)

    load_lengths.start()
    for g in range(GROUPS):
        own_copy(g, 0).start()
        own_copy(g, 1).start()
    load_query.start()
    load_grad.start()

    def piece(s):
        return (s,) if STREAMS > 1 else ()

    def forward(g, b, s, up):
        here = kv.at[(g, b) + piece(s)]
        return pltpu.make_async_remote_copy(
            src_ref=here, dst_ref=here, send_sem=(up_out if up else down_out).at[g, b, s],
            recv_sem=kv_in.at[g, b, s], device_id=(dp, above if up else below), device_id_type=MESH,
        )

    def back(source, g, b, s, up, last=False):
        at = (g, b) + piece(s)
        return pltpu.make_async_remote_copy(
            src_ref=source.at[at],
            dst_ref=second.at[(g,) + piece(s)] if last else partial.at[at],
            send_sem=part_out.at[g, b, s],
            recv_sem=second_in.at[g, s] if last else part_in.at[g, b, s],
            device_id=(dp, above if up else below), device_id_type=MESH,
        )

    def add_own(g, b, s):
        at = (g, b) + piece(s)
        partial[at] = partial[at] + terms[at]

    def step(kind, place, b, s, g):
        if kind == OWN_UP:
            forward(g, b, s, True).start()
        elif kind == OWN_DOWN:
            forward(g, b, s, False).start()
        elif kind == FROM_BELOW:
            forward(g, b, s, True).wait_recv()
            if place - b < UP[s][b]:
                forward(g, b, s, True).start()
        elif kind == FROM_ABOVE:
            forward(g, b, s, False).wait_recv()
            if (b - place) % RING < DOWN[s][b]:
                forward(g, b, s, False).start()
        elif kind == END_UP:
            back(terms, g, b, s, False).start()
        elif kind == END_DOWN:
            back(terms, g, b, s, True, (b - place) % RING == 1).start()
        elif kind == BACK_DOWN:
            back(partial, g, b, s, False).wait_recv()
            add_own(g, b, s)
            back(partial, g, b, s, False).start()
        elif kind == BACK_UP:
            back(partial, g, b, s, True).wait_recv()
            if place > b:
                add_own(g, b, s)
            back(partial, g, b, s, True, (b - place) % RING == 1).start()
        else:
            at = (g, b) + piece(s)
            total = terms[at].astype(F32)
            if UP[s][b]:
                back(partial, g, b, s, False).wait_recv()
                total = total + partial[at].astype(F32)
            if DOWN[s][b]:
                back(partial, g, b, s, True, True).wait_recv()
                total = total + second[(g,) + piece(s)].astype(F32)
            dkv_out[(g,) + piece(s)] = total.astype(BF16)

    def sent(g):
        for place in range(RING):
            @pl.when(z == place)
            def _(place=place):
                for entry in [entry for part in PLAN[place] for entry in part]:
                    kind, b = entry[:2]
                    s = entry[3] if STREAMS > 1 else 0
                    if kind == OWN_UP or (kind == FROM_BELOW and place - b < UP[s][b]):
                        forward(g, b, s, True).wait_send()
                    elif kind == OWN_DOWN or (
                        kind == FROM_ABOVE and (b - place) % RING < DOWN[s][b]
                    ):
                        forward(g, b, s, False).wait_send()
                    elif kind in (END_UP, BACK_DOWN, END_DOWN, BACK_UP):
                        back(partial, g, b, s, kind in (END_DOWN, BACK_UP)).wait_send()

    def attend(g, part):
        keys = kv[g, :, 0].reshape(PACK, DEPTH)
        values = kv[g, :, 1].reshape(PACK, DEPTH)
        count = REPEAT // PARTS
        heads = [columns(g * REPEAT + part * count + h, DEPTH) for h in range(count)]
        queries = jnp.concatenate([query[:, c] for c in heads], axis=0)
        grads = jnp.concatenate([grad[:, c] for c in heads], axis=0)
        scores = product(keys, queries, 1, 1) + jnp.concatenate([bias[...]] * count, axis=1)
        row_max = jnp.max(scores, axis=0, keepdims=True)
        raised = jnp.exp2((scores - row_max) * EXP2_SCALE)
        inverse = 1.0 / jnp.sum(raised, axis=0, keepdims=True)
        weights = raised.astype(BF16)
        attn_out = (product(values, weights, 0, 0) * inverse).T.astype(BF16)
        grads = (grads.astype(F32) * jnp.broadcast_to(inverse, (DEPTH, count * ROWS)).T).astype(BF16)
        delta = jnp.sum(grads.astype(F32) * attn_out.astype(F32), axis=1, keepdims=True)
        delta = jnp.broadcast_to(delta, (count * ROWS, DEPTH)).T[:1]
        dscore = (product(values, grads, 1, 1) - delta).astype(BF16) * weights
        dqueries = (product(keys, dscore, 0, 0).T * SCALE).astype(BF16)
        for h, c in enumerate(heads):
            out[:, c] = attn_out[h * ROWS:(h + 1) * ROWS]
            dquery[:, c] = dqueries[h * ROWS:(h + 1) * ROWS]
        key_terms = product(dscore, queries, 1, 0)
        value_terms = product(weights, grads, 1, 0)
        if part:
            key_terms = key_terms + dkv[0]
            value_terms = value_terms + dkv[1]
        if part < PARTS - 1:
            dkv[0] = key_terms
            dkv[1] = value_terms
        else:
            terms[g, :, 0] = (key_terms * SCALE).astype(BF16).reshape(RING, ROWS, DEPTH)
            terms[g, :, 1] = value_terms.astype(BF16).reshape(RING, ROWS, DEPTH)

    def prepare():
        for s in range(STREAMS):
            for b in range(1, RING):
                if not DOWN[s][b]:
                    @pl.when(z < b)
                    def _(b=b, s=s):
                        for g in range(GROUPS):
                            at = (g, b) + piece(s)
                            kv[at] = jnp.zeros(kv.at[at].shape, BF16)

        load_lengths.wait()
        row_pos = z * ROWS + lax.broadcasted_iota(jnp.int32, (PACK, ROWS), 1)
        col_pos = lax.broadcasted_iota(jnp.int32, (PACK, ROWS), 0)
        row_doc = jnp.zeros((PACK, ROWS), jnp.int32)
        col_doc = jnp.zeros((PACK, ROWS), jnp.int32)
        end = jnp.int32(0)
        for k in range(DOCS):
            end = end + lengths[k, dp]
            row_doc = row_doc + (row_pos >= end).astype(jnp.int32)
            col_doc = col_doc + (col_pos >= end).astype(jnp.int32)
        bias[...] = jnp.where((row_doc == col_doc) & (col_pos <= row_pos), 0.0, NEGATIVE)

    def in_range(g):
        return (g >= 0) & (g < GROUPS)

    def tick(index, _):
        t = index + FIRST_TICK

        @pl.when(t == -1)
        def _():
            prepare()

        @pl.when(t == 0)
        def _():
            load_query.wait()
            load_grad.wait()

        for part in range(PARTS):
            @pl.when(in_range(t))
            def _(part=part):
                attend(t, part)

            for place in range(RING):
                @pl.when(z == place)
                def _(part=part, place=place):
                    for entry in PLAN[place][part]:
                        kind, b, offset = entry[:3]

                        @pl.when(in_range(t - offset))
                        def _(entry=entry, kind=kind, b=b, offset=offset):
                            step(kind, place, b, entry[3] if STREAMS > 1 else 0, t - offset)

        return 0

    for g in range(GROUPS):
        own_copy(g, 0).wait()
        own_copy(g, 1).wait()
    pl.semaphore_wait(barrier, 2)

    lax.fori_loop(0, LAST_TICK + 1 - FIRST_TICK, tick, 0)

    def finish(g, _):
        sent(g)
        return 0

    lax.fori_loop(0, GROUPS, finish, 0)


def store(out, dquery, dkv, out_hbm, dquery_hbm, dkey_hbm, dvalue_hbm, sem):
    copies = [
        pltpu.make_async_copy(out, out_hbm, sem.at[0]),
        pltpu.make_async_copy(dquery, dquery_hbm, sem.at[1]),
    ]
    for g in range(GROUPS):
        place = pl.ds(g * DEPTH, DEPTH)
        for which, target in enumerate((dkey_hbm, dvalue_hbm)):
            copies.append(pltpu.make_async_copy(
                dkv.at[g, which], target.at[:, place], sem.at[2 + 2 * g + which]
            ))
    for copy in copies:
        copy.start()
    for copy in copies:
        copy.wait()


def body(query_input, key_input, value_input, output_gradient, document_lengths):
    hbm = pl.BlockSpec(memory_space=pltpu.HBM)
    wide = jax.ShapeDtypeStruct((ROWS, GROUPS * WIDE), BF16)
    narrow = jax.ShapeDtypeStruct((ROWS, GROUPS * DEPTH), BF16)
    rows = pltpu.VMEM((ROWS, GROUPS * WIDE), BF16)
    blocks = pltpu.VMEM((GROUPS, RING, 2, ROWS, DEPTH), BF16)
    gathered = pltpu.VMEM((GROUPS, 2, ROWS, DEPTH), BF16)
    sems = pltpu.SemaphoreType.DMA
    each = sems((GROUPS, RING, STREAMS))
    inputs = [
        pltpu.with_memory_space_constraint(x, pltpu.HBM)
        for x in (query_input, key_input, value_input, output_gradient, document_lengths.T)
    ]
    held = pl.pallas_call(
        kernel,
        out_shape=(rows, rows, gathered),
        in_specs=[hbm] * 5,
        out_specs=(pl.BlockSpec(memory_space=pltpu.VMEM),) * 3,
        scratch_shapes=[
            pltpu.SMEM((DOCS, PACKS), jnp.int32),
            rows, rows,
            blocks, blocks, blocks, gathered,
            pltpu.VMEM((PACK, ROWS), F32),
            pltpu.VMEM((2, PACK, DEPTH), F32),
            each, each, each, each, sems((GROUPS, STREAMS)), each,
            sems((3,)), sems((GROUPS, 2)),
        ],
        compiler_params=pltpu.CompilerParams(
            collective_id=0, has_side_effects=True, vmem_limit_bytes=48 * 2**20
        ),
    )(*inputs)
    return pl.pallas_call(
        store,
        out_shape=(wide, wide, narrow, narrow),
        in_specs=[pl.BlockSpec(memory_space=pl.ANY)] * 3,
        out_specs=(hbm,) * 4,
        scratch_shapes=[sems((2 + 2 * GROUPS,))],
        compiler_params=pltpu.CompilerParams(vmem_limit_bytes=2**20),
    )(*held)


def solution(mesh):
    rows = P(("dp", "tensor"), None)
    return jax.shard_map(
        body,
        mesh=mesh,
        in_specs=(rows, rows, rows, rows, P()),
        out_specs=(rows, rows, rows, rows),
        check_vma=False,
    )
```
